128 devices in a mesh: row: 16 (over x_lo, z, core), col: 8 (over y, x_hi).
Axes of the slice: x: 4 (x_hi: 2, x_lo: 2; x = x_hi * 2 + x_lo), y: 4, z: 4, core: 2. Of those that a mesh axis runs over, the one named last changes fastest.
Arguments:
- pair_rows: bfloat16 [2048, 4096, 128], P('row', 'col'), may hold values from -45 to 45
- pair_cols: bfloat16 [256, 4096, 128], P('row', 'col'), may hold values from -45 to 45
- ln_gain: float32 [128], replicated, may hold values from 0.1 to 1.9
- ln_bias: float32 [128], replicated, may hold values from -3 to 3
- left_weight: bfloat16 [128, 256], replicated, may hold values from -0.5 to 0.5
- right_weight: bfloat16 [128, 256], replicated, may hold values from -0.5 to 0.5
- gate_weight: bfloat16 [128, 128], replicated, may hold values from -0.5 to 0.5
- out_gain: float32 [128], replicated, may hold values from 0.1 to 1.9
- out_bias: float32 [128], replicated, may hold values from -3 to 3
- out_weight: bfloat16 [128, 128], replicated, may hold values from -0.5 to 0.5
Outputs:
- update: bfloat16 [2048, 256, 128], P('row', 'col')
The draws below stay inside these ranges and needn't reach their ends.
All inputs are finite; a program needn't handle non-finite values.
Results may differ from the reference program's by a relative error of at most 0.018.
Values may be sent and summed in bfloat16 or wider, within the bound.
No kernel may reach another device: no remote copies, remote signals or barrier semaphores. Data moves between devices by JAX's collectives and lax.ppermute only.
A program may use at most 320 MiB of HBM per device.

```python
import jax
import jax.numpy as jnp
from jax import lax

C = 128
CH = 128
KTOK = 4096
ROWS_DEV = 128
COLS_DEV = 32
ROWS = 2048
COLS = 256
N_ROW = 16
N_COL = 8


def draw_pair_rows(key, part):
    key = jax.random.fold_in(key, 11)
    first, second = jax.random.split(key, 2)
    scales = jnp.exp(jax.random.uniform(first, (ROWS, KTOK, 1), jnp.float32) * jnp.log(10.0))
    base = jnp.clip(jax.random.normal(second, (ROWS, KTOK, C), jnp.float32), -4.0, 4.0)
    return (base * scales).astype(jnp.bfloat16)


def draw_pair_cols(key, part):
    key = jax.random.fold_in(key, 23)
    first, second = jax.random.split(key, 2)
    scales = jnp.exp(jax.random.uniform(first, (COLS, KTOK, 1), jnp.float32) * jnp.log(10.0))
    base = jnp.clip(jax.random.normal(second, (COLS, KTOK, C), jnp.float32), -4.0, 4.0)
    return (base * scales).astype(jnp.bfloat16)


def gaussian(key, shape, scale, most, kind=jnp.bfloat16):
    drawn = jax.random.normal(key, shape, jnp.float32) * scale
    return jnp.minimum(jnp.maximum(drawn, -most), most).astype(kind)


def setup_inputs(seed: int = 0) -> dict:
    key_list = jax.random.split(jax.random.key(seed), 11)
    return {
        "pair_rows": draw_pair_rows(jax.random.fold_in(key_list[10], 71), 0),
        "pair_cols": draw_pair_cols(jax.random.fold_in(key_list[10], 71), 0),
        "ln_gain": jnp.clip(1.0 + 0.18 * jax.random.normal(key_list[2], (C,), jnp.float32), 0.1, 1.9),
        "ln_bias": gaussian(key_list[3], (C,), 0.5, 3.0, jnp.float32),
        "left_weight": gaussian(key_list[4], (C, 2 * CH), C ** -0.5, 0.5),
        "right_weight": gaussian(key_list[5], (C, 2 * CH), C ** -0.5, 0.5),
        "gate_weight": gaussian(key_list[6], (C, C), C ** -0.5, 0.5),
        "out_gain": jnp.clip(1.0 + 0.18 * jax.random.normal(key_list[7], (CH,), jnp.float32), 0.1, 1.9),
        "out_bias": gaussian(key_list[8], (CH,), 0.5, 3.0, jnp.float32),
        "out_weight": gaussian(key_list[9], (CH, C), CH ** -0.5, 0.5),
    }


def normalize(values, gain, bias):
    values = values.astype(jnp.float32)
    center = lax.optimization_barrier(jnp.mean(values, axis=-1, keepdims=True))
    spread = lax.optimization_barrier(jnp.mean((values - center) ** 2, axis=-1, keepdims=True))
    return (values - center) * lax.rsqrt(spread + 1e-05) * gain + bias

def project_pair(normed, weight, width):
    normed_f = normed.astype(jnp.float32)
    weight_f = weight.astype(jnp.float32)
    gated = jnp.einsum('ikc,cd->ikd', normed_f, weight_f[:, :width])
    valued = jnp.einsum('ikc,cd->ikd', normed_f, weight_f[:, width:])
    return (jax.nn.sigmoid(gated) * valued).astype(jnp.bfloat16)

def reference(pair_rows, pair_cols, ln_gain, ln_bias, left_weight, right_weight, gate_weight, out_gain, out_bias, out_weight):
    normed_cols = normalize(pair_cols, ln_gain, ln_bias).astype(jnp.bfloat16)
    right_act = project_pair(normed_cols, right_weight, CH).astype(jnp.float32)
    places = jnp.arange(COLS, dtype=jnp.int32)
    tokens = places // COLS_DEV * (KTOK // N_COL) + places % COLS_DEV
    blocks = pair_rows.reshape(N_ROW, ROWS_DEV, KTOK, C)

    def one_block(block):
        normed = normalize(block, ln_gain, ln_bias).astype(jnp.bfloat16)
        left_act = project_pair(normed, left_weight, CH).astype(jnp.float32)
        product = jnp.einsum('ikh,jkh->ijh', left_act, right_act)
        window = jnp.take(normed, tokens, axis=1).astype(jnp.float32)
        gate = jax.nn.sigmoid(jnp.einsum('ijc,cd->ijd', window, gate_weight.astype(jnp.float32)))
        normed_product = normalize(product, out_gain, out_bias).astype(jnp.bfloat16)
        mixed = jnp.einsum('ijh,hd->ijd', normed_product.astype(jnp.float32), out_weight.astype(jnp.float32))
        return (gate * mixed).astype(jnp.bfloat16)
    result = lax.map(one_block, blocks)
    return result.reshape(ROWS, COLS, C)
```

```python
import functools

import jax
import jax.numpy as jnp
from jax import lax
from jax.experimental import pallas as pl
from jax.experimental.pallas import tpu as pltpu
from jax.sharding import PartitionSpec as P

F32, BF16 = jnp.float32, jnp.bfloat16
EPS = 1e-05
VMEM = 60 * 2**20
ANY = pl.BlockSpec(memory_space=pl.ANY)


def cost(us):
    return pl.CostEstimate(flops=int(us * 1.1e9), bytes_accessed=int(us * 3.2e6), transcendentals=0)


HALF = 64
COLS_DEV = 32
PART = 16
CHUNKS = (16, 24, 16, 8)
BH = 8
NT = (((1,), (1,)), ((), ()))
TN = (((0,), (0,)), ((), ()))


def pairs_of(move):
    pairs = []
    for r in range(16):
        for c in range(8):
            x, z, k, y, far = move(r // 8, (r // 2) % 4, r % 2, c // 2, c % 2)
            pairs.append((r * 8 + c, (x * 8 + z * 2 + k) * 8 + y * 2 + far))
    return pairs


def partner(flip, at):
    return flip * (3 - at) + (1 - flip) * (at + 1 - 2 * (at % 2))


SWAP_CORE = pairs_of(lambda x, z, k, y, far: (x, z, 1 - k, y, far))
SWAP_X = pairs_of(lambda x, z, k, y, far: (1 - x, z, k, y, far))
SWAP_FAR = pairs_of(lambda x, z, k, y, far: (x, z, k, y, 1 - far))
Z_FIRST = pairs_of(lambda x, z, k, y, far: (x, partner(k, z), k, y, far))
Z_SECOND = pairs_of(lambda x, z, k, y, far: (x, partner(1 - k, z), k, y, far))
Y_FIRST = pairs_of(lambda x, z, k, y, far: (x, z, k, partner(k, y), far))
Y_SECOND = pairs_of(lambda x, z, k, y, far: (x, z, k, partner(1 - k, y), far))


def send(value, pairs):
    return lax.ppermute(value, ("row", "col"), pairs)


def layer_norm(x, gain, bias):
    x = x.astype(F32)
    center = jnp.sum(x, axis=-1, keepdims=True) * (1.0 / 128)
    x = x - center
    spread = jnp.sum(x * x, axis=-1, keepdims=True) * (1.0 / 128)
    return (x * lax.rsqrt(spread + EPS) * gain + bias).astype(BF16)


def act_rows(weight, normed):
    acc = lax.dot_general(weight, normed, NT, preferred_element_type=F32)
    h = weight.shape[0] // 2
    return acc[h:] * (jnp.tanh(acc[:h]) + 1.0)


def spread_rows(scratch, t, act):
    for i in range(4):
        scratch[i, pl.ds(t, act.shape[0], stride=16), :] = act[:, 128 * i : 128 * i + 128]


def collect_rows(out, scratch, first):
    hc = out.shape[0]
    for i in range(4):
        part = scratch[i, first * 16 : (first + hc) * 16, :].astype(BF16)
        out[:, :, 128 * i : 128 * i + 128] = part.reshape(hc, 16, 128)


def right_kernel(core_ref, own_ref, got_ref, gain_ref, bias_ref, w_ref, *rest):
    outs, scratch = rest[:-1], rest[-1]
    mine = pl.program_id(0) == core_ref[0]

    def step(t, _):
        x = jnp.where(mine, own_ref[t], got_ref[t])
        act = act_rows(w_ref[...], layer_norm(x, gain_ref[...], bias_ref[...]))
        spread_rows(scratch, t, act)
        return 0

    lax.fori_loop(0, 16, step, 0, unroll=8)
    first = 0
    for out, hc in zip(outs, CHUNKS):
        collect_rows(out, scratch, first)
        first += hc


def right_call(core, own, got, gain, bias, weight):
    whole = lambda shape: pl.BlockSpec(shape, lambda t, s: (0,) * len(shape))
    return pl.pallas_call(
        right_kernel,
        grid_spec=pltpu.PrefetchScalarGridSpec(
            num_scalar_prefetch=1,
            grid=(2,),
            in_specs=[
                whole((16, 512, 128)),
                whole((16, 512, 128)),
                whole((1, 128)),
                whole((1, 128)),
                whole((128, 128)),
            ],
            out_specs=[
                pl.BlockSpec((hc, 16, 512), lambda t, s: (0, t, 0)) for hc in CHUNKS
            ],
            scratch_shapes=[pltpu.VMEM((4, HALF * 16, 128), F32)],
        ),
        out_shape=[jax.ShapeDtypeStruct((hc, 32, 512), BF16) for hc in CHUNKS],
        compiler_params=pltpu.CompilerParams(vmem_limit_bytes=VMEM),
        cost_estimate=cost(10),
        name="right",
    )(core, own, got, gain, bias, weight)


def left_kernel(n_passed, x_ref, gain_ref, bias_ref, w_ref, gw_ref, *rest):
    keep_ref, gate_ref, send_ref, scratch = *rest[-4 - n_passed : -1 - n_passed], rest[-1]
    half = pl.program_id(0) % 2

    def step(t, _):
        normed = layer_norm(x_ref[t], gain_ref[...], bias_ref[...])
        act = act_rows(w_ref[...], normed)
        spread_rows(scratch, half * 8 + t, act)
        gate = jnp.dot(normed[:COLS_DEV], gw_ref[...], preferred_element_type=F32)
        gate_ref[t] = jnp.tanh(gate) * 0.5 + 0.5
        return 0

    lax.fori_loop(0, 8, step, 0, unroll=8)

    @pl.when(half == 1)
    def _():
        collect_rows(keep_ref, scratch, 0)
        collect_rows(send_ref, scratch, HALF)


def left_call(part, rows, gain, bias, weight, gate_weight, so_far, passed, after):
    whole = lambda shape: pl.BlockSpec(shape, lambda t: (0,) * len(shape))
    n = rows.shape[0]
    base = part * PART
    operands = (*so_far, *passed, *after)
    aliases = {5 + i: i for i in range(len(so_far))}
    for i in range(len(passed)):
        aliases[5 + len(so_far) + i] = 3 + i
    return pl.pallas_call(
        functools.partial(left_kernel, len(passed)),
        grid=(PART // 8,),
        in_specs=[
            pl.BlockSpec((8, 512, 128), lambda t: (base // 8 + t, 0, 0)),
            whole((1, 128)),
            whole((1, 128)),
            whole((256, 128)),
            whole((128, 128)),
        ]
        + [ANY] * len(operands),
        out_specs=[
            pl.BlockSpec((HALF, 16, 512), lambda t: (0, base // 16 + t // 2, 0)),
            pl.BlockSpec((8, COLS_DEV, 128), lambda t: (base // 8 + t, 0, 0)),
            pl.BlockSpec((HALF, 16, 512), lambda t: (0, t // 2, 0)),
        ]
        + [ANY] * len(passed),
        out_shape=[
            jax.ShapeDtypeStruct((HALF, n, 512), BF16),
            jax.ShapeDtypeStruct((n, COLS_DEV, 128), F32),
            jax.ShapeDtypeStruct((HALF, PART, 512), BF16),
        ]
        + [jax.ShapeDtypeStruct(v.shape, v.dtype) for v in passed],
        input_output_aliases=aliases,
        scratch_shapes=[pltpu.VMEM((4, 128 * 16, 128), F32)],
        compiler_params=pltpu.CompilerParams(vmem_limit_bytes=VMEM),
        cost_estimate=cost(PART * 0.4),
        name="left",
    )(rows, gain, bias, weight, gate_weight, *operands)


def contract_kernel(slot_ref, *refs):
    shards, own, got, (near, far), scratch = refs[:4], refs[4], refs[5 : 5 + 128 // PART], refs[-3:-1], refs[-1]

    def step(h, _):
        right = jnp.concatenate([s[i, h] for s in shards for i in range(2)], axis=0)
        left = jnp.concatenate([own[h]] + [g[h] for g in got], axis=0)
        acc = lax.dot_general(right, left, NT, preferred_element_type=F32).astype(BF16)
        for s in range(8):
            scratch[slot_ref[s], h] = acc[32 * s : 32 * s + 32]
        return 0

    lax.fori_loop(0, BH, step, 0, unroll=4)
    near[...] = scratch[:4]
    far[...] = scratch[4:]


def contract_call(slots, shards, own, got, first, after):
    hc = shards[0].shape[1]
    base = first // BH
    return pl.pallas_call(
        contract_kernel,
        grid_spec=pltpu.PrefetchScalarGridSpec(
            num_scalar_prefetch=1,
            grid=(hc // BH,),
            in_specs=[pl.BlockSpec((2, BH, 32, 512), lambda t, s: (0, t, 0, 0))] * 4
            + [pl.BlockSpec((BH, 128, 512), lambda t, s: (base + t, 0, 0))]
            + [pl.BlockSpec((BH, PART, 512), lambda t, s: (base + t, 0, 0))] * len(got)
            + [ANY] * len(after),
            out_specs=[pl.BlockSpec((4, BH, 32, 256), lambda t, s: (0, t, 0, 0))] * 2,
            scratch_shapes=[pltpu.VMEM((8, BH, 32, 256), BF16)],
        ),
        out_shape=[jax.ShapeDtypeStruct((4, hc, 32, 256), BF16)] * 2,
        compiler_params=pltpu.CompilerParams(vmem_limit_bytes=VMEM),
        cost_estimate=cost(hc * 0.33),
        name="contract",
    )(slots, *shards, own, *got, *after)


def final_kernel(gain_ref, bias_ref, own_ref, got_ref, gate_ref, w_ref, out_ref, p_ref, o_ref):
    own = own_ref[...]
    got = got_ref[...].astype(F32)
    center = (jnp.sum(own, axis=0) + jnp.sum(got, axis=0)) * (1.0 / 128)
    spread = jnp.sum((own - center) ** 2, axis=0) + jnp.sum((got - center) ** 2, axis=0)
    scale = lax.rsqrt(spread * (1.0 / 128) + EPS)
    for h in range(128):
        part = own_ref[h] if h < HALF else got_ref[h - HALF].astype(F32)
        p_ref[32 * h : 32 * h + 32, :] = (part - center) * scale * gain_ref[h] + bias_ref[h]
    for q in range(COLS_DEV):
        normed = p_ref[pl.ds(q, 128, stride=32), :].T.astype(BF16)
        mixed = jnp.dot(normed, w_ref[...], preferred_element_type=F32)
        o_ref[pl.ds(q, 128, stride=32), :] = mixed
    out_ref[...] = (o_ref[...].reshape(128, COLS_DEV, 128) * gate_ref[...]).astype(BF16)


def final_call(gain, bias, own, got, gate, weight):
    vmem = pl.BlockSpec(memory_space=pltpu.VMEM)
    smem = pl.BlockSpec(memory_space=pltpu.SMEM)
    return pl.pallas_call(
        final_kernel,
        in_specs=[smem, smem, vmem, vmem, vmem, vmem],
        out_specs=vmem,
        out_shape=jax.ShapeDtypeStruct((128, COLS_DEV, 128), BF16),
        scratch_shapes=[pltpu.VMEM((128 * COLS_DEV, 128), F32)] * 2,
        compiler_params=pltpu.CompilerParams(vmem_limit_bytes=VMEM),
        name="final",
    )(gain, bias, own, got, gate, weight)


def scatter(near, far):
    got = send(far, Y_FIRST)
    passed = (near[2:].astype(F32) + got[2:].astype(F32)).astype(BF16)
    got_second = send(passed, Y_SECOND)
    total = near[:2].astype(F32) + got[:2].astype(F32) + got_second.astype(F32)
    crossed = send(total[1].astype(BF16), SWAP_FAR)
    return total[0] + crossed.astype(F32)


def body(
    pair_rows,
    pair_cols,
    ln_gain,
    ln_bias,
    left_weight,
    right_weight,
    gate_weight,
    out_gain,
    out_bias,
    out_weight,
):
    row, col = lax.axis_index("row"), lax.axis_index("col")
    core, z, x = row % 2, (row // 2) % 4, row // 8
    y, far = col // 2, col % 2

    def halves(v, axis):
        low, high = jnp.split(v, 2, axis)
        return jnp.where(core == 0, low, high), jnp.where(core == 0, high, low)

    gate_r, value_r = jnp.split(right_weight, 2, 1)
    gate_l, value_l = jnp.split(left_weight, 2, 1)
    w_right = jnp.concatenate([halves(gate_r, 1)[0], halves(value_r, 1)[0]], 1).T * 0.5
    w_left = jnp.concatenate([*halves(gate_l, 1), *halves(value_l, 1)], 1).T * 0.5
    gain_out = jnp.concatenate(halves(out_gain, 0))
    bias_out = jnp.concatenate(halves(out_bias, 0))
    w_out = jnp.concatenate(halves(out_weight, 0))
    gain, bias = ln_gain[None], ln_bias[None]
    w_right, w_left = w_right.astype(BF16), w_left.astype(BF16)
    gate_half = (gate_weight * 0.5).astype(BF16)

    first_y, second_y = partner(core, y), partner(1 - core, y)
    slots = []
    for zs in (z, partner(1 - core, z)):
        for xs in (x, 1 - x):
            for zt in (zs, partner(core, zs)):
                owner = 4 * xs + zt
                oy, of = owner // 2, owner % 2
                near = jnp.where(oy == y, 0, 2)
                beyond = jnp.where(oy == first_y, 4, 6)
                side = jnp.where((oy == y) | (oy == second_y), near, beyond)
                slots.append(side + (of ^ far))
    slots = jnp.stack(slots).astype(jnp.int32)

    got_cols = send(pair_cols, SWAP_CORE)
    shards = right_call(
        core.astype(jnp.int32)[None], pair_cols, got_cols, gain, bias, w_right
    )
    def first_step(own):
        return jnp.stack([own, send(own, Z_FIRST)])

    pairs = [first_step(shards[0]), first_step(shards[1])]
    others = [send(pairs[0], SWAP_X)]
    left, got = (), []
    later = list(shards[2:])
    for part in range(128 // PART):
        after = {0: [shards[0]], 1: [pairs[0]], 2: [pairs[1]]}.get(part, [])
        if part == 3:
            pairs += [first_step(v) for v in later]
        if part == 4:
            after = [pairs[2]]
            others.append(send(pairs[1], SWAP_X))
        if part == 5:
            after = [others[0], pairs[3]]
        passed = later if part == 1 else []
        keep, gate, sent, *handed = left_call(
            part, pair_rows, gain, bias, w_left, gate_half, left, passed, after
        )
        left = (keep, gate)
        later = handed or later
        got.append(send(sent, SWAP_CORE))
    others += [send(pair, SWAP_X) for pair in pairs[2:]]
    shards_of = [
        [pair, other, send(pair, Z_SECOND), send(other, Z_SECOND)]
        for pair, other in zip(pairs, others)
    ]
    totals = []
    first = 0
    for i, hc in enumerate(CHUNKS):
        after = [others[i + 1]] if i + 1 < len(CHUNKS) else []
        near, beyond = contract_call(slots, shards_of[i], keep, got, first, after)
        totals.append(scatter(near, beyond))
        first += hc
    total = jnp.concatenate(totals, 0)
    other = send(total[:, :, 128:].astype(BF16), SWAP_CORE)
    return final_call(gain_out, bias_out, total[:, :, :128], other, gate, w_out)


def solution(mesh):
    return jax.shard_map(
        body,
        mesh=mesh,
        in_specs=(P("row", "col", None),) * 2 + (P(),) * 8,
        out_specs=P("row", "col", None),
        check_vma=False,
    )
```

```python
import functools

import jax
import jax.numpy as jnp
from jax import lax
from jax.experimental import pallas as pl
from jax.experimental.pallas import tpu as pltpu
from jax.sharding import PartitionSpec as P

F32, BF16 = jnp.float32, jnp.bfloat16
EPS = 1e-05
VMEM = 16 * 2**20
ANY = pl.BlockSpec(memory_space=pl.ANY)


def cost(us):
    return pl.CostEstimate(flops=int(us * 1.1e9), bytes_accessed=int(us * 3.2e6), transcendentals=0)


HALF = 64
COLS_DEV = 32
PART = 16
GROUPS = (1,) * 8
CHUNKS = (16, 16, 24, 8)
BH = 8
NT = (((1,), (1,)), ((), ()))
TN = (((0,), (0,)), ((), ()))


def pairs_of(move):
    pairs = []
    for r in range(16):
        for c in range(8):
            x, z, k, y, far = move(r // 8, (r // 2) % 4, r % 2, c // 2, c % 2)
            pairs.append((r * 8 + c, (x * 8 + z * 2 + k) * 8 + y * 2 + far))
    return pairs


def partner(flip, at):
    return flip * (3 - at) + (1 - flip) * (at + 1 - 2 * (at % 2))


SWAP_CORE = pairs_of(lambda x, z, k, y, far: (x, z, 1 - k, y, far))
SWAP_X = pairs_of(lambda x, z, k, y, far: (1 - x, z, k, y, far))
SWAP_FAR = pairs_of(lambda x, z, k, y, far: (x, z, k, y, 1 - far))
Z_FIRST = pairs_of(lambda x, z, k, y, far: (x, partner(k, z), k, y, far))
Z_SECOND = pairs_of(lambda x, z, k, y, far: (x, partner(1 - k, z), k, y, far))
Y_FIRST = pairs_of(lambda x, z, k, y, far: (x, z, k, partner(k, y), far))
Y_SECOND = pairs_of(lambda x, z, k, y, far: (x, z, k, partner(1 - k, y), far))


def send(value, pairs):
    return lax.ppermute(value, ("row", "col"), pairs)


def layer_norm(x, gain, bias):
    x = x.astype(F32)
    center = jnp.sum(x, axis=-1, keepdims=True) * (1.0 / 128)
    x = x - center
    spread = jnp.sum(x * x, axis=-1, keepdims=True) * (1.0 / 128)
    return (x * lax.rsqrt(spread + EPS) * gain + bias).astype(BF16)


def act_rows(weight, normed):
    acc = lax.dot_general(weight, normed, NT, preferred_element_type=F32)
    h = weight.shape[0] // 2
    return acc[h:] * (jnp.tanh(acc[:h]) + 1.0)


def spread_rows(scratch, t, act):
    for i in range(4):
        scratch[i, pl.ds(t, act.shape[0], stride=16), :] = act[:, 128 * i : 128 * i + 128]


def collect_rows(out, scratch, first):
    hc = out.shape[0]
    for i in range(4):
        part = scratch[i, first * 16 : (first + hc) * 16, :].astype(BF16)
        out[:, :, 128 * i : 128 * i + 128] = part.reshape(hc, 16, 128)


def right_kernel(core_ref, own_ref, got_ref, gain_ref, bias_ref, w_ref, *rest):
    outs, scratch = rest[:-1], rest[-1]
    mine = pl.program_id(0) == core_ref[0]

    def step(t, _):
        x = jnp.where(mine, own_ref[t], got_ref[t])
        act = act_rows(w_ref[...], layer_norm(x, gain_ref[...], bias_ref[...]))
        spread_rows(scratch, t, act)
        return 0

    lax.fori_loop(0, 16, step, 0, unroll=8)
    first = 0
    for out in outs:
        hc = out.shape[0]
        collect_rows(out, scratch, first)
        first += hc


def right_call(core, own, got, gain, bias, weight):
    whole = lambda shape: pl.BlockSpec(shape, lambda t, s: (0,) * len(shape))
    return pl.pallas_call(
        right_kernel,
        grid_spec=pltpu.PrefetchScalarGridSpec(
            num_scalar_prefetch=1,
            grid=(2,),
            in_specs=[
                whole((16, 512, 128)),
                whole((16, 512, 128)),
                whole((1, 128)),
                whole((1, 128)),
                whole((128, 128)),
            ],
            out_specs=[
                pl.BlockSpec((hc, 16, 512), lambda t, s: (0, t, 0)) for hc in (CHUNKS[0], HALF - CHUNKS[0])
            ],
            scratch_shapes=[pltpu.VMEM((4, HALF * 16, 128), F32)],
        ),
        out_shape=[jax.ShapeDtypeStruct((hc, 32, 512), BF16) for hc in (CHUNKS[0], HALF - CHUNKS[0])],
        compiler_params=pltpu.CompilerParams(vmem_limit_bytes=24 * 2**20),
        cost_estimate=cost(10),
        name="right",
    )(core, own, got, gain, bias, weight)


def left_kernel(x_ref, gain_ref, bias_ref, w_ref, *rest):
    keep_ref, send_ref, scratch = rest[-3:]
    half = pl.program_id(0) % 2

    def step(t, _):
        normed = layer_norm(x_ref[t], gain_ref[...], bias_ref[...])
        act = act_rows(w_ref[...], normed)
        spread_rows(scratch, half * 8 + t, act)
        return 0

    lax.fori_loop(0, 8, step, 0, unroll=8)

    @pl.when(half == 1)
    def _():
        collect_rows(keep_ref, scratch, 0)
        collect_rows(send_ref, scratch, HALF)


def left_call(part, place, group, rows, gain, bias, weight, so_far, after):
    whole = lambda shape: pl.BlockSpec(shape, lambda t: (0,) * len(shape))
    n = rows.shape[0]
    base = part * PART
    operands = (*so_far, *after)
    aliases = {4 + i: i for i in range(len(so_far))}
    return pl.pallas_call(
        left_kernel,
        grid=(PART // 8,),
        in_specs=[
            pl.BlockSpec((8, 512, 128), lambda t: (base // 8 + t, 0, 0)),
            whole((1, 128)),
            whole((1, 128)),
            whole((256, 128)),
        ]
        + [ANY] * len(operands),
        out_specs=[
            pl.BlockSpec((HALF, 16, 512), lambda t: (0, base // 16 + t // 2, 0)),
            pl.BlockSpec((HALF, 16, 512), lambda t: (0, place + t // 2, 0)),
        ],
        out_shape=[
            jax.ShapeDtypeStruct((HALF, n, 512), BF16),
            jax.ShapeDtypeStruct((HALF, group * PART, 512), BF16),
        ],
        input_output_aliases=aliases,
        scratch_shapes=[pltpu.VMEM((4, 128 * 16, 128), F32)],
        compiler_params=pltpu.CompilerParams(vmem_limit_bytes=VMEM),
        cost_estimate=cost(PART * 0.4),
        name="left",
    )(rows, gain, bias, weight, *operands)


def gate_kernel(x_ref, gain_ref, bias_ref, gw_ref, _, gate_ref):
    normed = layer_norm(x_ref[...].reshape(-1, 128), gain_ref[...], bias_ref[...])
    gate = jnp.dot(normed, gw_ref[...], preferred_element_type=F32)
    gate_ref[...] = (jnp.tanh(gate) * 0.5 + 0.5).reshape(gate_ref.shape)


def gate_call(rows, gain, bias, gate_weight, after):
    n = rows.shape[0]
    whole = lambda shape: pl.BlockSpec(shape, lambda t: (0,) * len(shape))
    return pl.pallas_call(
        gate_kernel,
        grid=(n // 32,),
        in_specs=[
            pl.BlockSpec((32, COLS_DEV, 128), lambda t: (t, 0, 0)),
            whole((1, 128)),
            whole((1, 128)),
            whole((128, 128)),
            ANY,
        ],
        out_specs=pl.BlockSpec((32, COLS_DEV, 128), lambda t: (t, 0, 0)),
        out_shape=jax.ShapeDtypeStruct((n, COLS_DEV, 128), F32),
        compiler_params=pltpu.CompilerParams(vmem_limit_bytes=VMEM),
        cost_estimate=cost(14),
        name="gate",
    )(rows, gain, bias, gate_weight, after)


def contract_kernel(n_in, slot_ref, *refs):
    shards, own, got = refs[:4], refs[4], refs[5 : 5 + len(GROUPS)]
    near, far, scratch = *refs[n_in : n_in + 2], refs[-1]

    def step(h, _):
        right = jnp.concatenate([s[i, h] for s in shards for i in range(2)], axis=0)
        left = jnp.concatenate([own[h]] + [g[h] for g in got], axis=0)
        acc = lax.dot_general(right, left, NT, preferred_element_type=F32).astype(BF16)
        for s in range(8):
            scratch[slot_ref[s], h] = acc[32 * s : 32 * s + 32]
        return 0

    lax.fori_loop(0, BH, step, 0, unroll=4)
    near[...] = scratch[:4]
    far[...] = scratch[4:]


def contract_call(slots, shards, own, got, first, after, passed):
    hc = shards[0].shape[1]
    base = first // BH
    operands = (*shards, own, *got, *after, *passed)
    n_in = len(operands)
    aliases = {1 + n_in - len(passed) + i: 2 + i for i in range(len(passed))}
    return pl.pallas_call(
        functools.partial(contract_kernel, n_in),
        grid_spec=pltpu.PrefetchScalarGridSpec(
            num_scalar_prefetch=1,
            grid=(hc // BH,),
            in_specs=[pl.BlockSpec((2, BH, 32, 512), lambda t, s: (0, t, 0, 0))] * 4
            + [pl.BlockSpec((BH, 128, 512), lambda t, s: (base + t, 0, 0))]
            + [pl.BlockSpec((BH, g.shape[1], 512), lambda t, s: (base + t, 0, 0)) for g in got]
            + [ANY] * (len(after) + len(passed)),
            out_specs=[pl.BlockSpec((4, BH, 32, 256), lambda t, s: (0, t, 0, 0))] * 2
            + [ANY] * len(passed),
            scratch_shapes=[pltpu.VMEM((8, BH, 32, 256), BF16)],
        ),
        out_shape=[jax.ShapeDtypeStruct((4, hc, 32, 256), BF16)] * 2
        + [jax.ShapeDtypeStruct(v.shape, v.dtype) for v in passed],
        input_output_aliases=aliases,
        compiler_params=pltpu.CompilerParams(vmem_limit_bytes=VMEM),
        cost_estimate=cost(hc * 0.33),
        name="contract",
    )(slots, *operands)


def final_kernel(gain_ref, bias_ref, own_ref, got_ref, gate_ref, w_ref, out_ref, p_ref, o_ref):
    own = own_ref[...]
    got = got_ref[...].astype(F32)
    center = (jnp.sum(own, axis=0) + jnp.sum(got, axis=0)) * (1.0 / 128)
    spread = jnp.sum((own - center) ** 2, axis=0) + jnp.sum((got - center) ** 2, axis=0)
    scale = lax.rsqrt(spread * (1.0 / 128) + EPS)
    for h in range(128):
        part = own_ref[h] if h < HALF else got_ref[h - HALF].astype(F32)
        p_ref[32 * h : 32 * h + 32, :] = (part - center) * scale * gain_ref[h] + bias_ref[h]
    for q in range(COLS_DEV):
        normed = p_ref[pl.ds(q, 128, stride=32), :].T.astype(BF16)
        mixed = jnp.dot(normed, w_ref[...], preferred_element_type=F32)
        o_ref[pl.ds(q, 128, stride=32), :] = mixed
    out_ref[...] = (o_ref[...].reshape(128, COLS_DEV, 128) * gate_ref[...]).astype(BF16)


def final_call(gain, bias, total, got, gate, weight):
    smem = pl.BlockSpec(memory_space=pltpu.SMEM)
    whole = lambda *shape: pl.BlockSpec(shape, lambda t: (0,) * len(shape))
    return pl.pallas_call(
        final_kernel,
        grid=(1,),
        in_specs=[
            smem,
            smem,
            whole(HALF, COLS_DEV, 128),
            whole(HALF, COLS_DEV, 128),
            whole(128, COLS_DEV, 128),
            whole(128, 128),
        ],
        out_specs=whole(128, COLS_DEV, 128),
        out_shape=jax.ShapeDtypeStruct((128, COLS_DEV, 128), BF16),
        scratch_shapes=[pltpu.VMEM((128 * COLS_DEV, 128), F32)] * 2,
        compiler_params=pltpu.CompilerParams(vmem_limit_bytes=24 * 2**20),
        name="final",
    )(gain, bias, total, got, gate, weight)


def scatter(near, far):
    got = send(far, Y_FIRST)
    passed = (near[2:].astype(F32) + got[2:].astype(F32)).astype(BF16)
    got_second = send(passed, Y_SECOND)
    total = near[:2].astype(F32) + got[:2].astype(F32) + got_second.astype(F32)
    crossed = send(total[1].astype(BF16), SWAP_FAR)
    return total[0] + crossed.astype(F32)


def body(
    pair_rows,
    pair_cols,
    ln_gain,
    ln_bias,
    left_weight,
    right_weight,
    gate_weight,
    out_gain,
    out_bias,
    out_weight,
):
    row, col = lax.axis_index("row"), lax.axis_index("col")
    core, z, x = row % 2, (row // 2) % 4, row // 8
    y, far = col // 2, col % 2

    def halves(v, axis):
        low, high = jnp.split(v, 2, axis)
        return jnp.where(core == 0, low, high), jnp.where(core == 0, high, low)

    gate_r, value_r = jnp.split(right_weight, 2, 1)
    gate_l, value_l = jnp.split(left_weight, 2, 1)
    w_right = jnp.concatenate([halves(gate_r, 1)[0], halves(value_r, 1)[0]], 1).T * 0.5
    w_left = jnp.concatenate([*halves(gate_l, 1), *halves(value_l, 1)], 1).T * 0.5
    gain_out = jnp.concatenate(halves(out_gain, 0))
    bias_out = jnp.concatenate(halves(out_bias, 0))
    w_out = jnp.concatenate(halves(out_weight, 0))
    gain, bias = ln_gain[None], ln_bias[None]
    w_right, w_left = w_right.astype(BF16), w_left.astype(BF16)
    gate_half = (gate_weight * 0.5).astype(BF16)

    first_y, second_y = partner(core, y), partner(1 - core, y)
    slots = []
    for zs in (z, partner(1 - core, z)):
        for xs in (x, 1 - x):
            for zt in (zs, partner(core, zs)):
                owner = 4 * xs + zt
                oy, of = owner // 2, owner % 2
                near = jnp.where(oy == y, 0, 2)
                beyond = jnp.where(oy == first_y, 4, 6)
                side = jnp.where((oy == y) | (oy == second_y), near, beyond)
                slots.append(side + (of ^ far))
    slots = jnp.stack(slots).astype(jnp.int32)

    got_cols = send(pair_cols, SWAP_CORE)
    shards = right_call(
        core.astype(jnp.int32)[None], pair_cols, got_cols, gain, bias, w_right
    )
    pairs = [jnp.stack([shards[0], send(shards[0], Z_FIRST)])]
    met = send(shards[1], Z_FIRST)
    first = 0
    for hc in CHUNKS[1:]:
        pairs.append(jnp.stack([v[first : first + hc] for v in (shards[1], met)]))
        first += hc
    others = [send(pairs[0], SWAP_X)]
    beside = [send(pairs[0], Z_SECOND)]
    past = []
    so_far, got = [], []
    places = [(place, n) for n in GROUPS for place in range(n)]
    for part, (place, group) in enumerate(places):
        after = {
            0: [shards[0]],
            1: pairs[:1],
            3: pairs[1:2],
            4: others[:1],
            5: pairs[2:4],
            6: past[:1] + beside[1:2],
            7: others[1:2] + [gain_out, bias_out, w_out],
        }.get(part, [])
        if part >= 2:
            after = after + [got[part - 2]]
        *so_far, sent = left_call(
            part, place, group, pair_rows, gain, bias, w_left, so_far, after
        )
        if place == group - 1:
            got.append(send(sent, SWAP_CORE))
        else:
            so_far.append(sent)
        if part == 3:
            others.append(send(pairs[1], SWAP_X))
            beside.append(send(pairs[1], Z_SECOND))
        if part == 4:
            past.append(send(others[0], Z_SECOND))
    (keep,) = so_far
    gate = gate_call(pair_rows, gain, bias, gate_half, sent)
    others.append(send(pairs[2], SWAP_X))
    beside.append(send(pairs[2], Z_SECOND))
    past += [send(other, Z_SECOND) for other in others[1:]]
    totals = []
    first = 0
    for i, hc in enumerate(CHUNKS):
        after = [[gate, past[1]], [], others[3:], []][i]
        passed = pairs[3:] if i == 0 else []
        four = [pairs[i], others[i], beside[i], past[i]]
        near, beyond, *handed = contract_call(slots, four, keep, got, first, after, passed)
        if handed:
            pairs[3:] = handed
            others.append(send(pairs[3], SWAP_X))
            beside.append(send(pairs[3], Z_SECOND))
            past.append(send(others[3], Z_SECOND))
        totals.append(scatter(near, beyond))
        first += hc
    total = jnp.concatenate(totals, 0)
    other = send(total[:, :, 128:].astype(BF16), SWAP_CORE)
    return final_call(gain_out, bias_out, total, other, gate, w_out)


def solution(mesh):
    return jax.shard_map(
        body,
        mesh=mesh,
        in_specs=(P("row", "col", None),) * 2 + (P(),) * 8,
        out_specs=P("row", "col", None),
        check_vma=False,
    )
```

```python
import functools

import jax
import jax.numpy as jnp
from jax import lax
from jax.experimental import pallas as pl
from jax.experimental.pallas import tpu as pltpu
from jax.sharding import PartitionSpec as P

F32, BF16 = jnp.float32, jnp.bfloat16
EPS = 1e-05
VMEM = 16 * 2**20
ANY = pl.BlockSpec(memory_space=pl.ANY)


def cost(us):
    return pl.CostEstimate(flops=int(us * 1.1e9), bytes_accessed=int(us * 3.2e6), transcendentals=0)


HALF = 64
COLS_DEV = 32
PART = 16
GROUPS = (1, 1, 1, 1, 1, 1, 2)
CHUNKS = (16, 16, 24, 8)
BH = 8
NT = (((1,), (1,)), ((), ()))
TN = (((0,), (0,)), ((), ()))


def pairs_of(move):
    pairs = []
    for r in range(16):
        for c in range(8):
            x, z, k, y, far = move(r // 8, (r // 2) % 4, r % 2, c // 2, c % 2)
            pairs.append((r * 8 + c, (x * 8 + z * 2 + k) * 8 + y * 2 + far))
    return pairs


def partner(flip, at):
    return flip * (3 - at) + (1 - flip) * (at + 1 - 2 * (at % 2))


SWAP_CORE = pairs_of(lambda x, z, k, y, far: (x, z, 1 - k, y, far))
SWAP_X = pairs_of(lambda x, z, k, y, far: (1 - x, z, k, y, far))
SWAP_FAR = pairs_of(lambda x, z, k, y, far: (x, z, k, y, 1 - far))
Z_FIRST = pairs_of(lambda x, z, k, y, far: (x, partner(k, z), k, y, far))
Z_SECOND = pairs_of(lambda x, z, k, y, far: (x, partner(1 - k, z), k, y, far))
Y_FIRST = pairs_of(lambda x, z, k, y, far: (x, z, k, partner(k, y), far))
Y_SECOND = pairs_of(lambda x, z, k, y, far: (x, z, k, partner(1 - k, y), far))


def send(value, pairs):
    return lax.ppermute(value, ("row", "col"), pairs)


def layer_norm(x, gain, bias):
    x = x.astype(F32)
    center = jnp.sum(x, axis=-1, keepdims=True) * (1.0 / 128)
    x = x - center
    spread = jnp.sum(x * x, axis=-1, keepdims=True) * (1.0 / 128)
    return (x * lax.rsqrt(spread + EPS) * gain + bias).astype(BF16)


def act_rows(weight, normed):
    acc = lax.dot_general(weight, normed, NT, preferred_element_type=F32)
    h = weight.shape[0] // 2
    return acc[h:] * (jnp.tanh(acc[:h]) + 1.0)


def spread_rows(scratch, t, act):
    for i in range(4):
        scratch[i, pl.ds(t, act.shape[0], stride=16), :] = act[:, 128 * i : 128 * i + 128]


def collect_rows(out, scratch, first):
    hc = out.shape[0]
    for i in range(4):
        part = scratch[i, first * 16 : (first + hc) * 16, :].astype(BF16)
        out[:, :, 128 * i : 128 * i + 128] = part.reshape(hc, 16, 128)


def right_kernel(core_ref, own_ref, got_ref, gain_ref, bias_ref, w_ref, *rest):
    outs, scratch = rest[:-1], rest[-1]
    mine = pl.program_id(0) == core_ref[0]

    def step(t, _):
        x = jnp.where(mine, own_ref[t], got_ref[t])
        act = act_rows(w_ref[...], layer_norm(x, gain_ref[...], bias_ref[...]))
        spread_rows(scratch, t, act)
        return 0

    lax.fori_loop(0, 16, step, 0, unroll=8)
    first = 0
    for out in outs:
        hc = out.shape[0]
        collect_rows(out, scratch, first)
        first += hc


def right_call(core, own, got, gain, bias, weight):
    whole = lambda shape: pl.BlockSpec(shape, lambda t, s: (0,) * len(shape))
    return pl.pallas_call(
        right_kernel,
        grid_spec=pltpu.PrefetchScalarGridSpec(
            num_scalar_prefetch=1,
            grid=(2,),
            in_specs=[
                whole((16, 512, 128)),
                whole((16, 512, 128)),
                whole((1, 128)),
                whole((1, 128)),
                whole((128, 128)),
            ],
            out_specs=[
                pl.BlockSpec((hc, 16, 512), lambda t, s: (0, t, 0)) for hc in (CHUNKS[0], HALF - CHUNKS[0])
            ],
            scratch_shapes=[pltpu.VMEM((4, HALF * 16, 128), F32)],
        ),
        out_shape=[jax.ShapeDtypeStruct((hc, 32, 512), BF16) for hc in (CHUNKS[0], HALF - CHUNKS[0])],
        compiler_params=pltpu.CompilerParams(vmem_limit_bytes=24 * 2**20),
        cost_estimate=cost(10),
        name="right",
    )(core, own, got, gain, bias, weight)


def left_kernel(x_ref, gain_ref, bias_ref, w_ref, *rest):
    keep_ref, send_ref, scratch = rest[-3:]
    half = pl.program_id(0) % 2

    def step(t, _):
        normed = layer_norm(x_ref[t], gain_ref[...], bias_ref[...])
        act = act_rows(w_ref[...], normed)
        spread_rows(scratch, half * 8 + t, act)
        return 0

    lax.fori_loop(0, 8, step, 0, unroll=8)

    @pl.when(half == 1)
    def _():
        collect_rows(keep_ref, scratch, 0)
        collect_rows(send_ref, scratch, HALF)


def left_call(part, place, group, rows, gain, bias, weight, so_far, after):
    whole = lambda shape: pl.BlockSpec(shape, lambda t: (0,) * len(shape))
    base = part * PART
    operands = (*so_far, *after)
    aliases = {4 + i: 1 + i for i in range(len(so_far))}
    return pl.pallas_call(
        left_kernel,
        grid=(PART // 8,),
        in_specs=[
            pl.BlockSpec((8, 512, 128), lambda t: (base // 8 + t, 0, 0)),
            whole((1, 128)),
            whole((1, 128)),
            whole((256, 128)),
        ]
        + [ANY] * len(operands),
        out_specs=[
            pl.BlockSpec((HALF, 16, 512), lambda t: (0, t // 2, 0)),
            pl.BlockSpec((HALF, 16, 512), lambda t: (0, place + t // 2, 0)),
        ],
        out_shape=[
            jax.ShapeDtypeStruct((HALF, PART, 512), BF16),
            jax.ShapeDtypeStruct((HALF, group * PART, 512), BF16),
        ],
        input_output_aliases=aliases,
        scratch_shapes=[pltpu.VMEM((4, 128 * 16, 128), F32)],
        compiler_params=pltpu.CompilerParams(vmem_limit_bytes=VMEM),
        cost_estimate=cost(PART * 0.4),
        name="left",
    )(rows, gain, bias, weight, *operands)


def gate_kernel(x_ref, gain_ref, bias_ref, gw_ref, _, gate_ref):
    normed = layer_norm(x_ref[...].reshape(-1, 128), gain_ref[...], bias_ref[...])
    gate = jnp.dot(normed, gw_ref[...], preferred_element_type=F32)
    gate_ref[...] = (jnp.tanh(gate) * 0.5 + 0.5).reshape(gate_ref.shape)


def gate_call(rows, gain, bias, gate_weight, after):
    n = rows.shape[0]
    whole = lambda shape: pl.BlockSpec(shape, lambda t: (0,) * len(shape))
    return pl.pallas_call(
        gate_kernel,
        grid=(n // 32,),
        in_specs=[
            pl.BlockSpec((32, COLS_DEV, 128), lambda t: (t, 0, 0)),
            whole((1, 128)),
            whole((1, 128)),
            whole((128, 128)),
            ANY,
        ],
        out_specs=pl.BlockSpec((32, COLS_DEV, 128), lambda t: (t, 0, 0)),
        out_shape=jax.ShapeDtypeStruct((n, COLS_DEV, 128), F32),
        compiler_params=pltpu.CompilerParams(vmem_limit_bytes=VMEM),
        cost_estimate=cost(24),
        name="gate",
    )(rows, gain, bias, gate_weight, after)


def contract_kernel(n_in, slot_ref, *refs):
    shards, lefts = refs[:4], refs[4 : 4 + 128 // PART + len(GROUPS)]
    near, far, scratch = *refs[n_in : n_in + 2], refs[-1]

    def step(h, _):
        right = jnp.concatenate([s[i, h] for s in shards for i in range(2)], axis=0)
        left = jnp.concatenate([v[h] for v in lefts], axis=0)
        acc = lax.dot_general(right, left, NT, preferred_element_type=F32).astype(BF16)
        for s in range(8):
            scratch[slot_ref[s], h] = acc[32 * s : 32 * s + 32]
        return 0

    lax.fori_loop(0, BH, step, 0, unroll=4)
    near[...] = scratch[:4]
    far[...] = scratch[4:]


def contract_call(slots, shards, lefts, first, after, passed):
    hc = shards[0].shape[1]
    base = first // BH
    operands = (*shards, *lefts, *after, *passed)
    n_in = len(operands)
    aliases = {1 + n_in - len(passed) + i: 2 + i for i in range(len(passed))}
    return pl.pallas_call(
        functools.partial(contract_kernel, n_in),
        grid_spec=pltpu.PrefetchScalarGridSpec(
            num_scalar_prefetch=1,
            grid=(hc // BH,),
            in_specs=[pl.BlockSpec((2, BH, 32, 512), lambda t, s: (0, t, 0, 0))] * 4
            + [pl.BlockSpec((BH, v.shape[1], 512), lambda t, s: (base + t, 0, 0)) for v in lefts]
            + [ANY] * (len(after) + len(passed)),
            out_specs=[pl.BlockSpec((4, BH, 32, 256), lambda t, s: (0, t, 0, 0))] * 2
            + [ANY] * len(passed),
            scratch_shapes=[pltpu.VMEM((8, BH, 32, 256), BF16)],
        ),
        out_shape=[jax.ShapeDtypeStruct((4, hc, 32, 256), BF16)] * 2
        + [jax.ShapeDtypeStruct(v.shape, v.dtype) for v in passed],
        input_output_aliases=aliases,
        compiler_params=pltpu.CompilerParams(vmem_limit_bytes=VMEM),
        cost_estimate=cost(hc * 0.33),
        name="contract",
    )(slots, *operands)


def final_kernel(gain_ref, bias_ref, own_ref, got_ref, gate_ref, w_ref, out_ref, p_ref, o_ref):
    own = own_ref[...]
    got = got_ref[...].astype(F32)
    center = (jnp.sum(own, axis=0) + jnp.sum(got, axis=0)) * (1.0 / 128)
    spread = jnp.sum((own - center) ** 2, axis=0) + jnp.sum((got - center) ** 2, axis=0)
    scale = lax.rsqrt(spread * (1.0 / 128) + EPS)
    for h in range(128):
        part = own_ref[h] if h < HALF else got_ref[h - HALF].astype(F32)
        p_ref[32 * h : 32 * h + 32, :] = (part - center) * scale * gain_ref[h] + bias_ref[h]
    for q in range(COLS_DEV):
        normed = p_ref[pl.ds(q, 128, stride=32), :].T.astype(BF16)
        mixed = jnp.dot(normed, w_ref[...], preferred_element_type=F32)
        o_ref[pl.ds(q, 128, stride=32), :] = mixed
    out_ref[...] = (o_ref[...].reshape(128, COLS_DEV, 128) * gate_ref[...]).astype(BF16)


def final_call(gain, bias, total, got, gate, weight):
    smem = pl.BlockSpec(memory_space=pltpu.SMEM)
    whole = lambda *shape: pl.BlockSpec(shape, lambda t: (0,) * len(shape))
    return pl.pallas_call(
        final_kernel,
        grid=(1,),
        in_specs=[
            smem,
            smem,
            whole(HALF, COLS_DEV, 128),
            whole(HALF, COLS_DEV, 128),
            whole(128, COLS_DEV, 128),
            whole(128, 128),
        ],
        out_specs=whole(128, COLS_DEV, 128),
        out_shape=jax.ShapeDtypeStruct((128, COLS_DEV, 128), BF16),
        scratch_shapes=[pltpu.VMEM((128 * COLS_DEV, 128), F32)] * 2,
        compiler_params=pltpu.CompilerParams(vmem_limit_bytes=24 * 2**20),
        name="final",
    )(gain, bias, total, got, gate, weight)


def scatter(near, far):
    got = send(far, Y_FIRST)
    passed = (near[2:].astype(F32) + got[2:].astype(F32)).astype(BF16)
    got_second = send(passed, Y_SECOND)
    total = near[:2].astype(F32) + got[:2].astype(F32) + got_second.astype(F32)
    crossed = send(total[1].astype(BF16), SWAP_FAR)
    return total[0] + crossed.astype(F32)


def body(
    pair_rows,
    pair_cols,
    ln_gain,
    ln_bias,
    left_weight,
    right_weight,
    gate_weight,
    out_gain,
    out_bias,
    out_weight,
):
    row, col = lax.axis_index("row"), lax.axis_index("col")
    core, z, x = row % 2, (row // 2) % 4, row // 8
    y, far = col // 2, col % 2

    def halves(v, axis):
        low, high = jnp.split(v, 2, axis)
        return jnp.where(core == 0, low, high), jnp.where(core == 0, high, low)

    gate_r, value_r = jnp.split(right_weight, 2, 1)
    gate_l, value_l = jnp.split(left_weight, 2, 1)
    w_right = jnp.concatenate([halves(gate_r, 1)[0], halves(value_r, 1)[0]], 1).T * 0.5
    w_left = jnp.concatenate([*halves(gate_l, 1), *halves(value_l, 1)], 1).T * 0.5
    gain_out = jnp.concatenate(halves(out_gain, 0))
    bias_out = jnp.concatenate(halves(out_bias, 0))
    w_out = jnp.concatenate(halves(out_weight, 0))
    gain, bias = ln_gain[None], ln_bias[None]
    w_right, w_left = w_right.astype(BF16), w_left.astype(BF16)
    gate_half = (gate_weight * 0.5).astype(BF16)

    first_y, second_y = partner(core, y), partner(1 - core, y)
    slots = []
    for zs in (z, partner(1 - core, z)):
        for xs in (x, 1 - x):
            for zt in (zs, partner(core, zs)):
                owner = 4 * xs + zt
                oy, of = owner // 2, owner % 2
                near = jnp.where(oy == y, 0, 2)
                beyond = jnp.where(oy == first_y, 4, 6)
                side = jnp.where((oy == y) | (oy == second_y), near, beyond)
                slots.append(side + (of ^ far))
    slots = jnp.stack(slots).astype(jnp.int32)

    got_cols = send(pair_cols, SWAP_CORE)
    shards = right_call(
        core.astype(jnp.int32)[None], pair_cols, got_cols, gain, bias, w_right
    )
    pairs = [jnp.stack([shards[0], send(shards[0], Z_FIRST)])]
    met = send(shards[1], Z_FIRST)
    first = 0
    for hc in CHUNKS[1:]:
        pairs.append(jnp.stack([v[first : first + hc] for v in (shards[1], met)]))
        first += hc
    others = [send(pairs[0], SWAP_X)]
    beside = [send(pairs[0], Z_SECOND)]
    past = []
    keep, so_far, got = [], [], []
    places = [(place, n) for n in GROUPS for place in range(n)]
    for part, (place, group) in enumerate(places):
        after = {
            0: [shards[0]],
            1: pairs[:1],
            3: pairs[1:2],
            4: others[:1],
            5: pairs[2:4],
            6: past[:1] + beside[1:2],
            7: others[1:2] + [gain_out, bias_out, w_out],
        }.get(part, [])
        if part >= 2:
            after = after + [got[part - 2]]
        kept, sent = left_call(
            part, place, group, pair_rows, gain, bias, w_left, so_far, after + keep[-1:]
        )
        keep.append(kept)
        so_far = [sent] if place < group - 1 else []
        if not so_far:
            got.append(send(sent, SWAP_CORE))
        if part == 3:
            others.append(send(pairs[1], SWAP_X))
            beside.append(send(pairs[1], Z_SECOND))
        if part == 4:
            past.append(send(others[0], Z_SECOND))
    gate = gate_call(pair_rows, gain, bias, gate_half, sent)
    others.append(send(pairs[2], SWAP_X))
    beside.append(send(pairs[2], Z_SECOND))
    past.append(send(others[1], Z_SECOND))
    totals = []
    first = 0
    for i, hc in enumerate(CHUNKS):
        after = [[gate], [], others[3:], []][i]
        passed = pairs[3:] + others[2:] if i == 0 else []
        four = [pairs[i], others[i], beside[i], past[i]]
        near, beyond, *handed = contract_call(slots, four, keep + got, first, after, passed)
        if handed:
            pairs[3], others[2] = handed
            past.append(send(others[2], Z_SECOND))
            others.append(send(pairs[3], SWAP_X))
            beside.append(send(pairs[3], Z_SECOND))
            past.append(send(others[3], Z_SECOND))
        totals.append(scatter(near, beyond))
        first += hc
    total = jnp.concatenate(totals, 0)
    other = send(total[:, :, 128:].astype(BF16), SWAP_CORE)
    return final_call(gain_out, bias_out, total, other, gate, w_out)


def solution(mesh):
    return jax.shard_map(
        body,
        mesh=mesh,
        in_specs=(P("row", "col", None),) * 2 + (P(),) * 8,
        out_specs=P("row", "col", None),
        check_vma=False,
    )
```

```python
import functools

import jax
import jax.numpy as jnp
from jax import lax
from jax.experimental import pallas as pl
from jax.experimental.pallas import tpu as pltpu
from jax.sharding import PartitionSpec as P

F32, BF16 = jnp.float32, jnp.bfloat16
EPS = 1e-05
VMEM = 16 * 2**20
ANY = pl.BlockSpec(memory_space=pl.ANY)


def cost(us):
    return pl.CostEstimate(flops=int(us * 1.1e9), bytes_accessed=int(us * 3.2e6), transcendentals=0)


HALF = 64
COLS_DEV = 32
PART = 16
GROUPS = (1, 1, 1, 1, 1, 1, 2)
CHUNKS = (16, 16, 24, 8)
BH = 8
NT = (((1,), (1,)), ((), ()))
TN = (((0,), (0,)), ((), ()))


def pairs_of(move):
    pairs = []
    for r in range(16):
        for c in range(8):
            x, z, k, y, far = move(r // 8, (r // 2) % 4, r % 2, c // 2, c % 2)
            pairs.append((r * 8 + c, (x * 8 + z * 2 + k) * 8 + y * 2 + far))
    return pairs


def partner(flip, at):
    return flip * (3 - at) + (1 - flip) * (at + 1 - 2 * (at % 2))


SWAP_CORE = pairs_of(lambda x, z, k, y, far: (x, z, 1 - k, y, far))
SWAP_X = pairs_of(lambda x, z, k, y, far: (1 - x, z, k, y, far))
SWAP_FAR = pairs_of(lambda x, z, k, y, far: (x, z, k, y, 1 - far))
Z_FIRST = pairs_of(lambda x, z, k, y, far: (x, partner(k, z), k, y, far))
Z_SECOND = pairs_of(lambda x, z, k, y, far: (x, partner(1 - k, z), k, y, far))
Y_FIRST = pairs_of(lambda x, z, k, y, far: (x, z, k, partner(k, y), far))
Y_SECOND = pairs_of(lambda x, z, k, y, far: (x, z, k, partner(1 - k, y), far))


def send(value, pairs):
    return lax.ppermute(value, ("row", "col"), pairs)


def layer_norm(x, gain, bias):
    x = x.astype(F32)
    center = jnp.sum(x, axis=-1, keepdims=True) * (1.0 / 128)
    x = x - center
    spread = jnp.sum(x * x, axis=-1, keepdims=True) * (1.0 / 128)
    return (x * lax.rsqrt(spread + EPS) * gain + bias).astype(BF16)


def act_rows(weight, normed):
    acc = lax.dot_general(weight, normed, NT, preferred_element_type=F32)
    h = weight.shape[0] // 2
    return acc[h:] * (jnp.tanh(acc[:h]) + 1.0)


def spread_rows(scratch, t, act):
    for i in range(4):
        scratch[i, pl.ds(t, act.shape[0], stride=16), :] = act[:, 128 * i : 128 * i + 128]


def collect_rows(out, scratch, first):
    hc = out.shape[0]
    for i in range(4):
        part = scratch[i, first * 16 : (first + hc) * 16, :].astype(BF16)
        out[:, :, 128 * i : 128 * i + 128] = part.reshape(hc, 16, 128)


def right_kernel(core_ref, own_ref, got_ref, gain_ref, bias_ref, w_ref, *rest):
    outs, scratch = rest[:-1], rest[-1]
    mine = pl.program_id(0) == core_ref[0]

    def step(t, _):
        x = jnp.where(mine, own_ref[t], got_ref[t])
        act = act_rows(w_ref[...], layer_norm(x, gain_ref[...], bias_ref[...]))
        spread_rows(scratch, t, act)
        return 0

    lax.fori_loop(0, 16, step, 0, unroll=8)
    first = 0
    for out in outs:
        hc = out.shape[0]
        collect_rows(out, scratch, first)
        first += hc


def right_call(core, own, got, gain, bias, weight):
    whole = lambda shape: pl.BlockSpec(shape, lambda t, s: (0,) * len(shape))
    return pl.pallas_call(
        right_kernel,
        grid_spec=pltpu.PrefetchScalarGridSpec(
            num_scalar_prefetch=1,
            grid=(2,),
            in_specs=[
                whole((16, 512, 128)),
                whole((16, 512, 128)),
                whole((1, 128)),
                whole((1, 128)),
                whole((128, 128)),
            ],
            out_specs=[
                pl.BlockSpec((hc, 16, 512), lambda t, s: (0, t, 0)) for hc in (CHUNKS[0], HALF - CHUNKS[0])
            ],
            scratch_shapes=[pltpu.VMEM((4, HALF * 16, 128), F32)],
        ),
        out_shape=[jax.ShapeDtypeStruct((hc, 32, 512), BF16) for hc in (CHUNKS[0], HALF - CHUNKS[0])],
        compiler_params=pltpu.CompilerParams(vmem_limit_bytes=24 * 2**20),
        cost_estimate=cost(10),
        name="right",
    )(core, own, got, gain, bias, weight)


def left_kernel(x_ref, gain_ref, bias_ref, w_ref, *rest):
    keep_ref, send_ref, scratch = rest[-3:]
    half = pl.program_id(0) % 2

    def step(t, _):
        normed = layer_norm(x_ref[t], gain_ref[...], bias_ref[...])
        act = act_rows(w_ref[...], normed)
        spread_rows(scratch, half * 8 + t, act)
        return 0

    lax.fori_loop(0, 8, step, 0, unroll=8)

    @pl.when(half == 1)
    def _():
        collect_rows(keep_ref, scratch, 0)
        collect_rows(send_ref, scratch, HALF)


def left_call(part, place, group, rows, gain, bias, weight, so_far, after):
    whole = lambda shape: pl.BlockSpec(shape, lambda t: (0,) * len(shape))
    base = part * PART
    operands = (*so_far, *after)
    aliases = {4 + i: 1 + i for i in range(len(so_far))}
    return pl.pallas_call(
        left_kernel,
        grid=(PART // 8,),
        in_specs=[
            pl.BlockSpec((8, 512, 128), lambda t: (base // 8 + t, 0, 0)),
            whole((1, 128)),
            whole((1, 128)),
            whole((256, 128)),
        ]
        + [ANY] * len(operands),
        out_specs=[
            pl.BlockSpec((HALF, 16, 512), lambda t: (0, t // 2, 0)),
            pl.BlockSpec((HALF, 16, 512), lambda t: (0, place + t // 2, 0)),
        ],
        out_shape=[
            jax.ShapeDtypeStruct((HALF, PART, 512), BF16),
            jax.ShapeDtypeStruct((HALF, group * PART, 512), BF16),
        ],
        input_output_aliases=aliases,
        scratch_shapes=[pltpu.VMEM((4, 128 * 16, 128), F32)],
        compiler_params=pltpu.CompilerParams(vmem_limit_bytes=VMEM),
        cost_estimate=cost(PART * 0.4),
        name="left",
    )(rows, gain, bias, weight, *operands)


def gate_kernel(x_ref, gain_ref, bias_ref, gw_ref, _, gate_ref):
    normed = layer_norm(x_ref[...].reshape(-1, 128), gain_ref[...], bias_ref[...])
    gate = jnp.dot(normed, gw_ref[...], preferred_element_type=F32)
    gate_ref[...] = (jnp.tanh(gate) * 0.5 + 0.5).reshape(gate_ref.shape)


def gate_call(rows, gain, bias, gate_weight, after):
    n = rows.shape[0]
    whole = lambda shape: pl.BlockSpec(shape, lambda t: (0,) * len(shape))
    return pl.pallas_call(
        gate_kernel,
        grid=(n // 32,),
        in_specs=[
            pl.BlockSpec((32, COLS_DEV, 128), lambda t: (t, 0, 0)),
            whole((1, 128)),
            whole((1, 128)),
            whole((128, 128)),
            ANY,
        ],
        out_specs=pl.BlockSpec((32, COLS_DEV, 128), lambda t: (t, 0, 0)),
        out_shape=jax.ShapeDtypeStruct((n, COLS_DEV, 128), F32),
        compiler_params=pltpu.CompilerParams(vmem_limit_bytes=VMEM),
        cost_estimate=cost(24),
        name="gate",
    )(rows, gain, bias, gate_weight, after)


def contract_kernel(n_in, slot_ref, *refs):
    shards, lefts = refs[:4], refs[4 : 4 + 128 // PART + len(GROUPS)]
    near, far, scratch = *refs[n_in : n_in + 2], refs[-1]

    def step(h, _):
        right = jnp.concatenate([s[i, h] for s in shards for i in range(2)], axis=0)
        left = jnp.concatenate([v[h] for v in lefts], axis=0)
        acc = lax.dot_general(right, left, NT, preferred_element_type=F32).astype(BF16)
        for s in range(8):
            scratch[slot_ref[s], h] = acc[32 * s : 32 * s + 32]
        return 0

    lax.fori_loop(0, BH, step, 0, unroll=4)
    near[...] = scratch[:4]
    far[...] = scratch[4:]


def contract_call(slots, shards, lefts, first, after, passed):
    hc = shards[0].shape[1]
    base = first // BH
    operands = (*shards, *lefts, *after, *passed)
    n_in = len(operands)
    aliases = {1 + n_in - len(passed) + i: 2 + i for i in range(len(passed))}
    return pl.pallas_call(
        functools.partial(contract_kernel, n_in),
        grid_spec=pltpu.PrefetchScalarGridSpec(
            num_scalar_prefetch=1,
            grid=(hc // BH,),
            in_specs=[pl.BlockSpec((2, BH, 32, 512), lambda t, s: (0, t, 0, 0))] * 4
            + [pl.BlockSpec((BH, v.shape[1], 512), lambda t, s: (base + t, 0, 0)) for v in lefts]
            + [ANY] * (len(after) + len(passed)),
            out_specs=[pl.BlockSpec((4, BH, 32, 256), lambda t, s: (0, t, 0, 0))] * 2
            + [ANY] * len(passed),
            scratch_shapes=[pltpu.VMEM((8, BH, 32, 256), BF16)],
        ),
        out_shape=[jax.ShapeDtypeStruct((4, hc, 32, 256), BF16)] * 2
        + [jax.ShapeDtypeStruct(v.shape, v.dtype) for v in passed],
        input_output_aliases=aliases,
        compiler_params=pltpu.CompilerParams(vmem_limit_bytes=VMEM),
        cost_estimate=cost(hc * 0.33),
        name="contract",
    )(slots, *operands)


def final_kernel(gain_ref, bias_ref, own_ref, got_ref, gate_ref, w_ref, out_ref, p_ref, o_ref):
    own = own_ref[...]
    got = got_ref[...].astype(F32)
    center = (jnp.sum(own, axis=0) + jnp.sum(got, axis=0)) * (1.0 / 128)
    spread = jnp.sum((own - center) ** 2, axis=0) + jnp.sum((got - center) ** 2, axis=0)
    scale = lax.rsqrt(spread * (1.0 / 128) + EPS)
    for h in range(128):
        part = own_ref[h] if h < HALF else got_ref[h - HALF].astype(F32)
        p_ref[32 * h : 32 * h + 32, :] = (part - center) * scale * gain_ref[h] + bias_ref[h]
    for q in range(COLS_DEV):
        normed = p_ref[pl.ds(q, 128, stride=32), :].T.astype(BF16)
        mixed = jnp.dot(normed, w_ref[...], preferred_element_type=F32)
        o_ref[pl.ds(q, 128, stride=32), :] = mixed
    out_ref[...] = (o_ref[...].reshape(128, COLS_DEV, 128) * gate_ref[...]).astype(BF16)


def final_call(gain, bias, total, got, gate, weight):
    smem = pl.BlockSpec(memory_space=pltpu.SMEM)
    whole = lambda *shape: pl.BlockSpec(shape, lambda t: (0,) * len(shape))
    return pl.pallas_call(
        final_kernel,
        grid=(1,),
        in_specs=[
            smem,
            smem,
            whole(HALF, COLS_DEV, 128),
            whole(HALF, COLS_DEV, 128),
            whole(128, COLS_DEV, 128),
            whole(128, 128),
        ],
        out_specs=whole(128, COLS_DEV, 128),
        out_shape=jax.ShapeDtypeStruct((128, COLS_DEV, 128), BF16),
        scratch_shapes=[pltpu.VMEM((128 * COLS_DEV, 128), F32)] * 2,
        compiler_params=pltpu.CompilerParams(vmem_limit_bytes=24 * 2**20),
        name="final",
    )(gain, bias, total, got, gate, weight)


def scatter(near, far):
    got = send(far, Y_FIRST)
    passed = (near[2:].astype(F32) + got[2:].astype(F32)).astype(BF16)
    got_second = send(passed, Y_SECOND)
    total = near[:2].astype(F32) + got[:2].astype(F32) + got_second.astype(F32)
    crossed = send(total[1].astype(BF16), SWAP_FAR)
    return total[0] + crossed.astype(F32)


def body(
    pair_rows,
    pair_cols,
    ln_gain,
    ln_bias,
    left_weight,
    right_weight,
    gate_weight,
    out_gain,
    out_bias,
    out_weight,
):
    row, col = lax.axis_index("row"), lax.axis_index("col")
    core, z, x = row % 2, (row // 2) % 4, row // 8
    y, far = col // 2, col % 2

    def halves(v, axis):
        low, high = jnp.split(v, 2, axis)
        return jnp.where(core == 0, low, high), jnp.where(core == 0, high, low)

    gate_r, value_r = jnp.split(right_weight, 2, 1)
    gate_l, value_l = jnp.split(left_weight, 2, 1)
    w_right = jnp.concatenate([halves(gate_r, 1)[0], halves(value_r, 1)[0]], 1).T * 0.5
    w_left = jnp.concatenate([*halves(gate_l, 1), *halves(value_l, 1)], 1).T * 0.5
    gain_out = jnp.concatenate(halves(out_gain, 0))
    bias_out = jnp.concatenate(halves(out_bias, 0))
    w_out = jnp.concatenate(halves(out_weight, 0))
    gain, bias = ln_gain[None], ln_bias[None]
    w_right, w_left = w_right.astype(BF16), w_left.astype(BF16)
    gate_half = (gate_weight * 0.5).astype(BF16)

    first_y, second_y = partner(core, y), partner(1 - core, y)
    slots = []
    for zs in (z, partner(1 - core, z)):
        for xs in (x, 1 - x):
            for zt in (zs, partner(core, zs)):
                owner = 4 * xs + zt
                oy, of = owner // 2, owner % 2
                near = jnp.where(oy == y, 0, 2)
                beyond = jnp.where(oy == first_y, 4, 6)
                side = jnp.where((oy == y) | (oy == second_y), near, beyond)
                slots.append(side + (of ^ far))
    slots = jnp.stack(slots).astype(jnp.int32)

    window = pair_rows[:, :COLS_DEV]
    got_cols = send(pair_cols, SWAP_CORE)
    shards = right_call(
        core.astype(jnp.int32)[None], pair_cols, got_cols, gain, bias, w_right
    )
    pairs = [jnp.stack([shards[0], send(shards[0], Z_FIRST)])]
    met = send(shards[1], Z_FIRST)
    first = 0
    for hc in CHUNKS[1:]:
        pairs.append(jnp.stack([v[first : first + hc] for v in (shards[1], met)]))
        first += hc
    others = [send(pairs[0], SWAP_X)]
    beside = [send(pairs[0], Z_SECOND)]
    past = []
    keep, so_far, got = [], [], []
    places = [(place, n) for n in GROUPS for place in range(n)]
    for part, (place, group) in enumerate(places):
        after = {
            0: [shards[0]],
            1: pairs[:1],
            3: pairs[1:2],
            4: others[:1],
            5: pairs[2:4],
            6: past[:1] + beside[1:2],
            7: others[1:2] + [gain_out, bias_out, w_out, window],
        }.get(part, [])
        if part >= 2:
            after = after + [got[part - 2]]
        kept, sent = left_call(
            part, place, group, pair_rows, gain, bias, w_left, so_far, after + keep[-1:]
        )
        keep.append(kept)
        so_far = [sent] if place < group - 1 else []
        if not so_far:
            got.append(send(sent, SWAP_CORE))
        if part == 3:
            others.append(send(pairs[1], SWAP_X))
            beside.append(send(pairs[1], Z_SECOND))
        if part == 4:
            past.append(send(others[0], Z_SECOND))
    gate = gate_call(window, gain, bias, gate_half, sent)
    others.append(send(pairs[2], SWAP_X))
    beside.append(send(pairs[2], Z_SECOND))
    past.append(send(others[1], Z_SECOND))
    totals = []
    first = 0
    for i, hc in enumerate(CHUNKS):
        after = [[gate], [], others[3:], []][i]
        passed = pairs[3:] + others[2:] if i == 0 else []
        four = [pairs[i], others[i], beside[i], past[i]]
        near, beyond, *handed = contract_call(slots, four, keep + got, first, after, passed)
        if handed:
            pairs[3], others[2] = handed
            past.append(send(others[2], Z_SECOND))
            others.append(send(pairs[3], SWAP_X))
            beside.append(send(pairs[3], Z_SECOND))
            past.append(send(others[3], Z_SECOND))
        totals.append(scatter(near, beyond))
        first += hc
    total = jnp.concatenate(totals, 0)
    other = send(total[:, :, 128:].astype(BF16), SWAP_CORE)
    return final_call(gain_out, bias_out, total, other, gate, w_out)


def solution(mesh):
    return jax.shard_map(
        body,
        mesh=mesh,
        in_specs=(P("row", "col", None),) * 2 + (P(),) * 8,
        out_specs=P("row", "col", None),
        check_vma=False,
    )
```
